128 devices in a mesh: seq: 32 (over z, y_lo, x), tp: 4 (over y_hi, core).
Axes of the slice: x: 4, y: 4 (y_hi: 2, y_lo: 2; y = y_hi * 2 + y_lo), z: 4, core: 2. Of those that a mesh axis runs over, the one named last changes fastest.
Arguments:
- hidden: bfloat16 [8192, 4096], P('seq', 'tp'), may hold values from -6 to 6
- ctx_weight: bfloat16 [4096, 1024], P('tp'), may hold values from -0.09375 to 0.09375
- codes: int32 [8192, 8], P(('seq', 'tp')), may hold values from 0 to 2047, as said below
- table: bfloat16 [2048, 1024], replicated, may hold values from -6 to 6
- qkv_weight: bfloat16 [1024, 3072], replicated, may hold values from -0.1875 to 0.1875
- out_weight: bfloat16 [1024, 1024], replicated, may hold values from -0.1875 to 0.1875
- cotangent: bfloat16 [8192, 8, 1024], P(('seq', 'tp')), may hold values from -6 to 6
Outputs:
- d_hidden: bfloat16 [8192, 4096], P('seq', 'tp')
- grad_ctx: float32 [4096, 1024], P('tp')
- grad_table: float32 [2048, 1024], P(('seq', 'tp'))
- grad_qkv: float32 [1024, 3072], P(('seq', 'tp'))
- grad_out: float32 [1024, 1024], P(('seq', 'tp'))
The draws below stay inside these ranges and needn't reach their ends.
Inputs may be any that keep to these rules, and one draw needn't show every extreme that they name: `codes`: split the ids into groups of 16 consecutive values starting at multiples of 16. Among the ids of one device (its 64 frames in order, 8 ids each), no group occurs more than 8 times, and one group occurs exactly 8 times among the ids of every device.
All inputs are finite; a program needn't handle non-finite values.
Results may differ from the reference program's by a relative error of at most 0.04.
Values may be sent and summed in bfloat16 or wider, within the bound.
No kernel may reach another device: no remote copies, remote signals or barrier semaphores. Data moves between devices by JAX's collectives and lax.ppermute only.
A program may use at most 128 MiB of HBM per device.

```python
import jax
import jax.numpy as jnp
from jax import lax

D = 4096
E = 1024
HEADS = 16
V = 2048
K = 8
TOK_DEV = 256
TOKENS = 8192
N_SEQ = 32
N_TP = 4


def draw_codes(key, part):
    key = jax.random.fold_in(key, 11)
    owners = N_SEQ * N_TP
    group_size = V // owners
    block_len = TOK_DEV // N_TP * K
    capacity = max(2, 2 * block_len // owners)
    other_slots = (owners - 1) * capacity
    key_full, key_slots, key_order, key_member = jax.random.split(key, 4)
    full_owner = jax.random.randint(key_full, (), 0, owners, dtype=jnp.int32)

    def one_block(slot_key, order_key):
        picked = jax.random.permutation(slot_key, other_slots)[:block_len - capacity].astype(jnp.int32)
        base_owner = picked // capacity
        shifted = base_owner + (base_owner >= full_owner).astype(jnp.int32)
        listed = jnp.concatenate([jnp.zeros((capacity,), jnp.int32) + full_owner, shifted])
        return listed[jax.random.permutation(order_key, block_len)]
    slot_keys = jax.random.split(key_slots, owners)
    order_keys = jax.random.split(key_order, owners)
    block_owners = jax.vmap(one_block)(slot_keys, order_keys)
    members = jax.random.randint(key_member, (owners, block_len), 0, group_size, dtype=jnp.int32)
    return (block_owners * group_size + members).reshape(TOKENS, K)


def shard_levels(key, extent, shards, smallest, top_value):
    level = 1.0
    for dim, parts in shards:
        heights = jax.random.uniform(jax.random.fold_in(jax.random.fold_in(key, 6), dim), (parts,), jnp.float32, smallest / len(shards), top_value / len(shards))
        level = level * jnp.repeat(jnp.exp(heights), extent[dim] // parts).reshape((-1,) + (1,) * (len(extent) - 1 - dim))
    return level


def gaussian(own_key, extent, scale, most, shards=(), kind=jnp.bfloat16):
    drawn = jax.random.normal(own_key, extent, jnp.float32) * scale
    if len(shards) > 0:
        drawn = shard_levels(own_key, extent, shards, -0.22, 0.18) * drawn
    return jnp.clip(drawn, min=-most, max=most).astype(kind)


def setup_inputs(seed: int = 0) -> dict:
    seeds = jax.random.split(jax.random.key(seed), 8)
    return {
        "hidden": gaussian(seeds[0], (TOKENS, D), 1.0, 6.0, ((0, 32), (1, 4))),
        "ctx_weight": gaussian(seeds[1], (D, E), D ** -0.5, 0.09375, ((0, 4),)),
        "codes": draw_codes(jax.random.fold_in(seeds[7], 71), 0),
        "table": gaussian(seeds[3], (V, E), 1.0, 6.0),
        "qkv_weight": gaussian(seeds[4], (E, 3 * E), E ** -0.5, 0.1875),
        "out_weight": gaussian(seeds[5], (E, E), E ** -0.5, 0.1875),
        "cotangent": gaussian(seeds[6], (TOKENS, K, E), 1.0, 6.0, ((0, 128),)),
    }


def embed(codes, table):
    vocab = table.shape[0]
    onehot = (codes.reshape(-1)[:, None] == jnp.arange(vocab, dtype=jnp.int32)[None, :]).astype(jnp.bfloat16)
    return jnp.dot(onehot, table, preferred_element_type=jnp.float32)

def depth_rest(context, embedded, qkv_weight, out_weight):
    frames = context.shape[0]
    width = context.shape[1]
    books = embedded.shape[0] // frames
    size = width // HEADS
    stream = (embedded.reshape(frames, books, width) + context.astype(jnp.float32)[:, None, :]).astype(jnp.bfloat16)
    flat = stream.reshape(frames * books, width)
    projected = jnp.dot(flat, qkv_weight.astype(jnp.bfloat16), preferred_element_type=jnp.float32).astype(jnp.bfloat16)
    projected = projected.reshape(frames, books, 3, HEADS, size).astype(jnp.float32)
    query, keys, values = (projected[:, :, 0], projected[:, :, 1], projected[:, :, 2])
    scores = jnp.einsum('fqhd,fkhd->fhqk', query, keys) / jnp.sqrt(jnp.float32(size))
    causal = jnp.arange(books)[:, None] >= jnp.arange(books)[None, :]
    weights = jnp.where(causal[None, None], jnp.exp(scores), jnp.float32(0.0))
    probs = (weights / lax.optimization_barrier(jnp.sum(weights, axis=-1, keepdims=True))).astype(jnp.bfloat16)
    mixed = jnp.einsum('fhqk,fkhd->fqhd', probs.astype(jnp.float32), values).astype(jnp.bfloat16)
    result = jnp.dot(mixed.reshape(frames * books, width), out_weight.astype(jnp.bfloat16), preferred_element_type=jnp.float32)
    return stream.astype(jnp.float32) + result.reshape(frames, books, width)

def reference(hidden, ctx_weight, codes, table, qkv_weight, out_weight, cotangent):
    context = jnp.dot(hidden, ctx_weight, preferred_element_type=jnp.float32).astype(jnp.bfloat16)
    embedded = embed(codes, table)
    unused, pull = jax.vjp(depth_rest, context, embedded, qkv_weight.astype(jnp.float32), out_weight.astype(jnp.float32))
    d_context, d_embedded, grad_qkv, grad_out = pull(cotangent.astype(jnp.float32))
    grad_table = jax.ops.segment_sum(d_embedded, codes.reshape(-1).astype(jnp.int32), num_segments=V)
    d_hidden = lax.dot_general(d_context, ctx_weight, (((1,), (1,)), ((), ())), preferred_element_type=jnp.float32).astype(jnp.bfloat16)
    grad_ctx = lax.dot_general(hidden, d_context, (((0,), (0,)), ((), ())), preferred_element_type=jnp.float32)
    return (d_hidden, grad_ctx, grad_table, grad_qkv, grad_out)
```

```python
import functools

import jax
import jax.numpy as jnp
from jax import lax
from jax.experimental import pallas as pl
from jax.experimental.pallas import tpu as pltpu
from jax.sharding import Mesh, PartitionSpec as P

HEADS = 16
BOOKS = 8
SIZE = 64
LANES = 128
BLOCK = 128

ALL = ("z", "yl", "x", "yh", "c")
CHIPS = ("z", "yl", "x", "yh")
SEQ = ("z", "yl", "x")
SWAP = [(0, 1), (1, 0)]
F32 = jnp.float32
BF16 = jnp.bfloat16


def dot(a, b, ca, cb):
    return lax.dot_general(a, b, (((ca,), (cb,)), ((), ())), preferred_element_type=F32)


def attention_kernel(proj_ref, d_mixed_ref, mixed_ref, d_proj_ref):
    half = d_mixed_ref.shape[1]
    row = lax.broadcasted_iota(jnp.int32, (2 * BLOCK, BLOCK), 0) % BLOCK
    col = lax.broadcasted_iota(jnp.int32, (2 * BLOCK, BLOCK), 1)
    visible = (row // BOOKS == col // BOOKS) & (col <= row)
    low = lax.broadcasted_iota(jnp.int32, (BLOCK, LANES), 1) < SIZE

    def stack(a):
        zero = jnp.zeros_like(a)
        return jnp.concatenate([jnp.where(low, a, zero), jnp.where(low, zero, a)], axis=0)

    def pick(a):
        return jnp.where(low, a[:BLOCK], a[BLOCK:])

    for pair in range(half // LANES):
        cols = slice(pair * LANES, (pair + 1) * LANES)
        kcols = slice(half + pair * LANES, half + (pair + 1) * LANES)
        vcols = slice(2 * half + pair * LANES, 2 * half + (pair + 1) * LANES)
        query = stack(proj_ref[:, cols])
        keys = proj_ref[:, kcols]
        values = proj_ref[:, vcols]
        d_mixed = stack(d_mixed_ref[:, cols])
        scores = dot(query, keys, 1, 1) * F32(0.125)
        weights = jnp.where(visible, jnp.exp(scores), F32(0.0))
        scale = F32(1.0) / jnp.sum(weights, axis=1, keepdims=True)
        exact = weights * scale
        probs = exact.astype(BF16)
        mixed_ref[:, cols] = pick(dot(probs, values, 1, 0)).astype(BF16)
        d_probs = dot(d_mixed, values, 1, 1).astype(BF16).astype(F32)
        inner = jnp.sum(d_probs * exact, axis=1, keepdims=True)
        d_scores = (exact * (d_probs - inner) * F32(0.125)).astype(BF16)
        d_proj_ref[:, cols] = pick(dot(d_scores, keys, 1, 0)).astype(BF16)
        d_proj_ref[:, kcols] = dot(d_scores, query, 0, 0).astype(BF16)
        d_proj_ref[:, vcols] = dot(probs, d_mixed, 0, 0).astype(BF16)


def attention(proj, d_mixed):
    tokens, wide = proj.shape
    half = d_mixed.shape[1]
    return pl.pallas_call(
        attention_kernel,
        grid=(tokens // BLOCK,),
        in_specs=[
            pl.BlockSpec((BLOCK, wide), lambda i: (i, 0)),
            pl.BlockSpec((BLOCK, half), lambda i: (i, 0)),
        ],
        out_specs=[
            pl.BlockSpec((BLOCK, half), lambda i: (i, 0)),
            pl.BlockSpec((BLOCK, wide), lambda i: (i, 0)),
        ],
        out_shape=[
            jax.ShapeDtypeStruct((tokens, half), BF16),
            jax.ShapeDtypeStruct((tokens, wide), BF16),
        ],
        compiler_params=pltpu.CompilerParams(vmem_limit_bytes=24 * 1024 * 1024),
        cost_estimate=pl.CostEstimate(
            flops=12 * tokens * BLOCK * 2 * half,
            bytes_accessed=2 * tokens * (wide + half) * 2,
            transcendentals=tokens * BLOCK * half // SIZE,
        ),
    )(proj, d_mixed)


def merge_kernel(cot_ref, mine_ref, other_ref, d_stream_ref, d_ctx_ref):
    d_flat = (mine_ref[...].astype(F32) + other_ref[...].astype(F32)).astype(BF16)
    d_stream = (cot_ref[...].astype(F32) + d_flat.astype(F32)).astype(BF16)
    d_stream_ref[...] = d_stream
    rows, width = d_stream.shape
    d_ctx = jnp.sum(d_stream.astype(F32).reshape(rows // BOOKS, BOOKS, width), axis=1)
    d_ctx_ref[...] = d_ctx.astype(BF16)


def merge(cot, mine, other):
    tokens, width = cot.shape
    steps = 4
    rows = tokens // steps
    spec = pl.BlockSpec((rows, width), lambda i: (i, 0))
    return pl.pallas_call(
        merge_kernel,
        grid=(steps,),
        in_specs=[spec, spec, pl.BlockSpec((rows, width), lambda i: ((i + steps // 2) % steps, 0))],
        out_specs=[spec, pl.BlockSpec((rows // BOOKS, width), lambda i: (i, 0))],
        out_shape=[
            jax.ShapeDtypeStruct((tokens, width), BF16),
            jax.ShapeDtypeStruct((tokens // BOOKS, width), BF16),
        ],
        compiler_params=pltpu.CompilerParams(vmem_limit_bytes=24 * 1024 * 1024),
        cost_estimate=pl.CostEstimate(
            flops=4 * tokens * width, bytes_accessed=8 * tokens * width, transcendentals=0
        ),
    )(cot, mine, other)


def scatter_sum(parts, axes):
    got = lax.all_to_all(parts, axes, 0, 0, tiled=False)
    return jnp.sum(got.astype(F32), axis=0)


def on_device(hidden, ctx_weight, codes, table, qkv_weight, out_weight, cotangent):
    core = lax.axis_index("c")
    yh = lax.axis_index("yh")
    width = ctx_weight.shape[1]
    half = width // 2
    frames = codes.shape[0]
    tokens = 2 * frames * BOOKS
    vocab = table.shape[0]

    swap = functools.partial(lax.ppermute, axis_name="c", perm=SWAP)
    ids = jnp.concatenate([codes, swap(codes)], axis=0).reshape(tokens)
    cot = cotangent.reshape(frames * BOOKS, width)
    cot = jnp.concatenate([cot, swap(cot)], axis=0)

    partial_ctx = dot(hidden, ctx_weight, 1, 0).astype(BF16).reshape(2, 2 * frames, width)
    away = lax.dynamic_index_in_dim(partial_ctx, 1 - yh, 0, keepdims=False)
    near = lax.dynamic_index_in_dim(partial_ctx, yh, 0, keepdims=False)
    chip_ctx = (near.astype(F32) + lax.ppermute(away, "yh", SWAP).astype(F32)).astype(BF16)
    context = (chip_ctx.astype(F32) + swap(chip_ctx).astype(F32)).astype(BF16)
    context = jnp.where(core == 0, context, jnp.roll(context, frames, axis=0))

    onehot = (ids[:, None] == jnp.arange(vocab, dtype=jnp.int32)[None, :]).astype(BF16)
    embedded = dot(onehot, table, 1, 0).astype(BF16)
    weight = lax.dynamic_index_in_dim(
        qkv_weight.reshape(width, 3, 2, half), core, 2, keepdims=False
    ).reshape(width, 3 * half)
    out_half = lax.dynamic_slice_in_dim(out_weight, core * half, half, 0)
    d_mixed = dot(cot, out_half, 1, 1).astype(BF16)

    stream = (
        embedded.astype(F32).reshape(2 * frames, BOOKS, width) + context.astype(F32)[:, None, :]
    ).astype(BF16).reshape(tokens, width)
    proj = dot(stream, weight, 1, 0).astype(BF16)
    mixed, d_proj = attention(proj, d_mixed)

    d_out = dot(mixed, cot, 0, 0).astype(BF16)
    d_flat = dot(d_proj, weight, 1, 1).astype(BF16)
    d_qkv = dot(stream, d_proj, 0, 0).astype(BF16)

    d_stream, d_ctx = merge(cot, d_flat, swap(d_flat))
    d_ctx = jnp.where(core == 0, d_ctx, jnp.roll(d_ctx, frames, axis=0))
    d_ctx_far = lax.ppermute(d_ctx, "yh", SWAP)
    d_ctx = jnp.where(
        yh == 0,
        jnp.concatenate([d_ctx, d_ctx_far], axis=0),
        jnp.concatenate([d_ctx_far, d_ctx], axis=0),
    )

    chips = 64
    d_out = d_out.reshape(2, 16, 2, 8, width).transpose(2, 0, 1, 3, 4).reshape(chips, 8, width)
    sum_out = scatter_sum(d_out, CHIPS)
    grad_out = lax.ppermute(
        sum_out, ("z", "c"), [(2 * z + c, 2 * (2 * c + z % 2) + z // 2) for z in range(4) for c in range(2)]
    )

    sum_qkv = scatter_sum(d_qkv.reshape(chips, 16, 3 * half), CHIPS)
    keep = lax.dynamic_slice_in_dim(sum_qkv, core * 8, 8, 0)
    give = lax.dynamic_slice_in_dim(sum_qkv, 8 - core * 8, 8, 0)
    take = swap(give)
    keep, take = keep.reshape(8, 3, 1, half), take.reshape(8, 3, 1, half)
    grad_qkv = jnp.where(
        core == 0, jnp.concatenate([keep, take], axis=2), jnp.concatenate([take, keep], axis=2)
    ).reshape(8, 6 * half)

    place = jnp.arange(vocab // 2, dtype=jnp.int32)
    rows = place // 16 * 32 + core * 16 + place % 16
    d_table = dot((rows[:, None] == ids[None, :]).astype(BF16), d_stream, 1, 0).astype(BF16)
    grad_table = scatter_sum(d_table.reshape(chips, 16, width), CHIPS)

    d_hidden = dot(d_ctx, ctx_weight, 1, 1).astype(BF16)
    ctx_part = dot(hidden, d_ctx, 0, 0).astype(BF16)
    ctx_sum = scatter_sum(ctx_part.reshape(32, 32, width), SEQ).astype(BF16)
    grad_ctx = lax.all_to_all(
        jnp.broadcast_to(ctx_sum[None], (32, 32, width)), SEQ, 0, 0, tiled=False
    ).reshape(32 * 32, width).astype(F32)
    return (d_hidden, grad_ctx, grad_table, grad_qkv, grad_out)


def solution(mesh):
    fine = Mesh(mesh.devices.reshape(4, 2, 4, 2, 2), ALL)
    in_specs = (
        P(SEQ, ("yh", "c")),
        P(("yh", "c"), None),
        P(ALL, None),
        P(),
        P(),
        P(),
        P(ALL, None, None),
    )
    out_specs = (
        P(SEQ, ("yh", "c")),
        P(("yh", "c"), None),
        P(ALL, None),
        P(ALL, None),
        P(ALL, None),
    )
    return jax.shard_map(
        on_device, mesh=fine, in_specs=in_specs, out_specs=out_specs, check_vma=False
    )
```

```python
import functools

import jax
import jax.numpy as jnp
from jax import lax
from jax.experimental import pallas as pl
from jax.experimental.pallas import tpu as pltpu
from jax.sharding import Mesh, PartitionSpec as P

HEADS = 16
BOOKS = 8
SIZE = 64
LANES = 128
BLOCK = 128

ALL = ("z", "yl", "x", "yh", "c")
CHIPS = ("z", "yl", "x", "yh")
SEQ = ("z", "yl", "x")
SWAP = [(0, 1), (1, 0)]
F32 = jnp.float32
BF16 = jnp.bfloat16


def dot(a, b, ca, cb):
    return lax.dot_general(a, b, (((ca,), (cb,)), ((), ())), preferred_element_type=F32)


def attend(query, keys, values, d_mixed):
    row = lax.broadcasted_iota(jnp.int32, (2 * BLOCK, BLOCK), 0) % BLOCK
    col = lax.broadcasted_iota(jnp.int32, (2 * BLOCK, BLOCK), 1)
    visible = (row // BOOKS == col // BOOKS) & (col <= row)
    low = lax.broadcasted_iota(jnp.int32, (BLOCK, LANES), 1) < SIZE

    def stack(a):
        zero = jnp.zeros_like(a)
        return jnp.concatenate([jnp.where(low, a, zero), jnp.where(low, zero, a)], axis=0)

    def pick(a):
        return jnp.where(low, a[:BLOCK], a[BLOCK:]).astype(BF16)

    query, d_mixed = stack(query), stack(d_mixed)
    scores = dot(query, keys, 1, 1) * F32(0.125)
    weights = jnp.where(visible, jnp.exp(scores), F32(0.0))
    exact = weights * (F32(1.0) / jnp.sum(weights, axis=1, keepdims=True))
    probs = exact.astype(BF16)
    mixed = pick(dot(probs, values, 1, 0))
    d_probs = dot(d_mixed, values, 1, 1).astype(BF16).astype(F32)
    inner = jnp.sum(d_probs * exact, axis=1, keepdims=True)
    d_scores = (exact * (d_probs - inner) * F32(0.125)).astype(BF16)
    d_query = pick(dot(d_scores, keys, 1, 0))
    d_keys = dot(d_scores, query, 0, 0).astype(BF16)
    d_values = dot(probs, d_mixed, 0, 0).astype(BF16)
    return mixed, d_query, d_keys, d_values


def block_kernel(
    core_ref, emb_ref, ctx_ref, cot_ref, wq_ref, wk_ref, wv_ref, wo_ref, d_flat_ref, grad_ref,
    proj, d_proj, d_mixed, mixed, acc_qkv, acc_out,
):
    step = pl.program_id(0)
    rows, width = emb_ref.shape
    half = wq_ref.shape[1]
    stream = (
        emb_ref[...].astype(F32).reshape(rows // BOOKS, BOOKS, width)
        + ctx_ref[...].astype(F32)[:, None, :]
    ).reshape(rows, width).astype(BF16)
    cot = cot_ref[...]
    for part, w_ref in enumerate((wq_ref, wk_ref, wv_ref)):
        proj[:, part * half : (part + 1) * half] = dot(stream, w_ref[...], 1, 0).astype(BF16)
    d_mixed[...] = dot(cot, wo_ref[...], 1, 1).astype(BF16)
    for block in range(rows // BLOCK):
        at = slice(block * BLOCK, (block + 1) * BLOCK)
        for pair in range(half // LANES):
            q = slice(pair * LANES, (pair + 1) * LANES)
            k = slice(half + pair * LANES, half + (pair + 1) * LANES)
            v = slice(2 * half + pair * LANES, 2 * half + (pair + 1) * LANES)
            mixed[at, q], d_proj[at, q], d_proj[at, k], d_proj[at, v] = attend(
                proj[at, q], proj[at, k], proj[at, v], d_mixed[at, q]
            )
    d_flat = dot(d_proj[:, :half], wq_ref[...], 1, 1)
    d_flat += dot(d_proj[:, half : 2 * half], wk_ref[...], 1, 1)
    d_flat += dot(d_proj[:, 2 * half :], wv_ref[...], 1, 1)
    d_flat_ref[...] = d_flat.astype(BF16)

    @pl.when(step == 0)
    def _():
        acc_qkv[...] = dot(stream, d_proj[...], 0, 0)
        acc_out[...] = dot(mixed[...], cot, 0, 0)

    @pl.when(step > 0)
    def _():
        acc_qkv[...] += dot(stream, d_proj[...], 0, 0)
        acc_out[...] += dot(mixed[...], cot, 0, 0)

    @pl.when(step == pl.num_programs(0) - 1)
    def _():
        grad_ref[:, : 3 * half] = acc_qkv[...].astype(BF16)
        for chip in range(width // 16):
            source = (chip % 32) * 2 + chip // 32
            own = acc_out[source * 8 : (source + 1) * 8, :]
            grad_ref[chip * 16 : (chip + 1) * 16, 3 * half :] = jnp.concatenate(
                [own[:, :half], own[:, half:]], axis=0
            ).astype(BF16)


def block(core, embedded, context, cot, qkv_weight, out_weight):
    tokens, width = cot.shape
    half = width // 2
    steps = 4
    rows = tokens // steps
    tall = pl.BlockSpec((rows, width), lambda i, c: (i, 0))

    def third(part):
        return pl.BlockSpec((width, half), lambda i, c: (0, 2 * part + c[0]))

    return pl.pallas_call(
        block_kernel,
        grid_spec=pltpu.PrefetchScalarGridSpec(
            num_scalar_prefetch=1,
            grid=(steps,),
            in_specs=[
                tall,
                pl.BlockSpec((rows // BOOKS, width), lambda i, c: (i, 0)),
                tall,
                third(0),
                third(1),
                third(2),
                pl.BlockSpec((half, width), lambda i, c: (c[0], 0)),
            ],
            out_specs=[tall, pl.BlockSpec((width, 2 * width), lambda i, c: (0, 0))],
            scratch_shapes=[
                pltpu.VMEM((rows, 3 * half), BF16),
                pltpu.VMEM((rows, 3 * half), BF16),
                pltpu.VMEM((rows, half), BF16),
                pltpu.VMEM((rows, half), BF16),
                pltpu.VMEM((width, 3 * half), F32),
                pltpu.VMEM((half, width), F32),
            ],
        ),
        out_shape=[
            jax.ShapeDtypeStruct((tokens, width), BF16),
            jax.ShapeDtypeStruct((width, 2 * width), BF16),
        ],
        compiler_params=pltpu.CompilerParams(vmem_limit_bytes=48 * 1024 * 1024),
        cost_estimate=pl.CostEstimate(
            flops=22 * tokens * width * width // 2,
            bytes_accessed=20 * 1024 * 1024,
            transcendentals=tokens * BLOCK * half // SIZE,
        ),
    )(core, embedded, context, cot, qkv_weight, qkv_weight, qkv_weight, out_weight)


def merge_kernel(core_ref, ids_ref, cot_ref, mine_ref, other_ref, d_table_ref, d_ctx_ref, acc):
    step = pl.program_id(0)
    d_flat = (mine_ref[...].astype(F32) + other_ref[...].astype(F32)).astype(BF16)
    d_stream = (cot_ref[...].astype(F32) + d_flat.astype(F32)).astype(BF16)
    rows, width = d_stream.shape
    d_ctx = jnp.sum(d_stream.astype(F32).reshape(rows // BOOKS, BOOKS, width), axis=1)
    d_ctx_ref[...] = d_ctx.astype(BF16)
    place = lax.broadcasted_iota(jnp.int32, (acc.shape[0], rows), 0)
    row = place // 16 * 32 + core_ref[0] * 16 + place % 16
    onehot = jnp.where(row == ids_ref[...], F32(1.0), F32(0.0)).astype(BF16)
    part = dot(onehot, d_stream, 1, 0)

    @pl.when(step == 0)
    def _():
        acc[...] = part

    @pl.when(step > 0)
    def _():
        acc[...] += part

    @pl.when(step == pl.num_programs(0) - 1)
    def _():
        d_table_ref[...] = acc[...].astype(BF16)


def merge(core, ids, cot, mine, other, vocab):
    tokens, width = cot.shape
    steps = 4
    rows = tokens // steps
    spec = pl.BlockSpec((rows, width), lambda i, c: (i, 0))
    return pl.pallas_call(
        merge_kernel,
        grid_spec=pltpu.PrefetchScalarGridSpec(
            num_scalar_prefetch=1,
            grid=(steps,),
            in_specs=[
                pl.BlockSpec((1, rows), lambda i, c: (0, i)),
                spec,
                spec,
                pl.BlockSpec((rows, width), lambda i, c: ((i + steps // 2) % steps, 0)),
            ],
            out_specs=[
                pl.BlockSpec((vocab // 2, width), lambda i, c: (0, 0)),
                pl.BlockSpec((rows // BOOKS, width), lambda i, c: (i, 0)),
            ],
            scratch_shapes=[pltpu.VMEM((vocab // 2, width), F32)],
        ),
        out_shape=[
            jax.ShapeDtypeStruct((vocab // 2, width), BF16),
            jax.ShapeDtypeStruct((tokens // BOOKS, width), BF16),
        ],
        compiler_params=pltpu.CompilerParams(vmem_limit_bytes=32 * 1024 * 1024),
        cost_estimate=pl.CostEstimate(
            flops=tokens * width * vocab, bytes_accessed=9 * tokens * width, transcendentals=0
        ),
    )(core, ids, cot, mine, other)


def scatter_sum(parts, axes):
    got = lax.all_to_all(parts, axes, 0, 0, tiled=False)
    return jnp.sum(got.astype(F32), axis=0)


def on_device(hidden, ctx_weight, codes, table, qkv_weight, out_weight, cotangent):
    core = lax.axis_index("c")
    yh = lax.axis_index("yh")
    width = ctx_weight.shape[1]
    half = width // 2
    frames = codes.shape[0]
    tokens = 2 * frames * BOOKS
    vocab = table.shape[0]

    swap = functools.partial(lax.ppermute, axis_name="c", perm=SWAP)
    ids = jnp.concatenate([codes, swap(codes)], axis=0).reshape(tokens)
    cot = cotangent.reshape(frames * BOOKS, width)
    cot = jnp.concatenate([cot, swap(cot)], axis=0)

    partial_ctx = dot(hidden, ctx_weight, 1, 0).astype(BF16).reshape(2, 2 * frames, width)
    away = lax.dynamic_index_in_dim(partial_ctx, 1 - yh, 0, keepdims=False)
    near = lax.dynamic_index_in_dim(partial_ctx, yh, 0, keepdims=False)
    chip_ctx = (near.astype(F32) + lax.ppermute(away, "yh", SWAP).astype(F32)).astype(BF16)
    context = (chip_ctx.astype(F32) + swap(chip_ctx).astype(F32)).astype(BF16)
    context = jnp.where(core == 0, context, jnp.roll(context, frames, axis=0))

    onehot = (ids[:, None] == jnp.arange(vocab, dtype=jnp.int32)[None, :]).astype(BF16)
    embedded = dot(onehot, table, 1, 0).astype(BF16)
    which = core.astype(jnp.int32).reshape(1)
    d_flat, grads = block(which, embedded, context, cot, qkv_weight, out_weight)
    d_table, d_ctx = merge(which, ids.reshape(1, tokens), cot, d_flat, swap(d_flat), vocab)
    d_ctx = jnp.where(core == 0, d_ctx, jnp.roll(d_ctx, frames, axis=0))
    d_ctx_far = lax.ppermute(d_ctx, "yh", SWAP)
    d_ctx = jnp.where(
        yh == 0,
        jnp.concatenate([d_ctx, d_ctx_far], axis=0),
        jnp.concatenate([d_ctx_far, d_ctx], axis=0),
    )

    chips = 64
    sums = scatter_sum(grads.reshape(chips, 16, 2 * width), CHIPS)
    sum_out = jnp.concatenate([sums[:8, 3 * half :], sums[8:, 3 * half :]], axis=1)
    grad_out = lax.ppermute(
        sum_out, ("z", "c"), [(2 * z + c, 2 * (2 * c + z % 2) + z // 2) for z in range(4) for c in range(2)]
    )
    sum_qkv = sums[:, : 3 * half]
    keep = lax.dynamic_slice_in_dim(sum_qkv, core * 8, 8, 0)
    give = lax.dynamic_slice_in_dim(sum_qkv, 8 - core * 8, 8, 0)
    take = swap(give)
    keep, take = keep.reshape(8, 3, 1, half), take.reshape(8, 3, 1, half)
    grad_qkv = jnp.where(
        core == 0, jnp.concatenate([keep, take], axis=2), jnp.concatenate([take, keep], axis=2)
    ).reshape(8, 6 * half)

    grad_table = scatter_sum(d_table.reshape(chips, 16, width), CHIPS)

    d_hidden = dot(d_ctx, ctx_weight, 1, 1).astype(BF16)
    ctx_part = dot(hidden, d_ctx, 0, 0).astype(BF16)
    ctx_sum = scatter_sum(ctx_part.reshape(32, 32, width), SEQ).astype(BF16)
    grad_ctx = lax.all_to_all(
        jnp.broadcast_to(ctx_sum[None], (32, 32, width)), SEQ, 0, 0, tiled=False
    ).reshape(32 * 32, width).astype(F32)
    return (d_hidden, grad_ctx, grad_table, grad_qkv, grad_out)


def solution(mesh):
    fine = Mesh(mesh.devices.reshape(4, 2, 4, 2, 2), ALL)
    in_specs = (
        P(SEQ, ("yh", "c")),
        P(("yh", "c"), None),
        P(ALL, None),
        P(),
        P(),
        P(),
        P(ALL, None, None),
    )
    out_specs = (
        P(SEQ, ("yh", "c")),
        P(("yh", "c"), None),
        P(ALL, None),
        P(ALL, None),
        P(ALL, None),
    )
    return jax.shard_map(
        on_device, mesh=fine, in_specs=in_specs, out_specs=out_specs, check_vma=False
    )
```

```python
import functools

import jax
import jax.numpy as jnp
from jax import lax
from jax.experimental import pallas as pl
from jax.experimental.pallas import tpu as pltpu
from jax.sharding import Mesh, PartitionSpec as P

HEADS = 16
BOOKS = 8
SIZE = 64
LANES = 128
BLOCK = 128

ALL = ("z", "yl", "x", "yh", "c")
SEQ = ("z", "yl", "x")
SWAP = [(0, 1), (1, 0)]

CHIPS = (("z", 4), ("yl", 2), ("x", 4), ("yh", 2))
RINGS = {"x": ("x",), "y": ("yl", "yh"), "z": ("z",)}
RING_ORDER = ("x", "y", "z")
F32 = jnp.float32
BF16 = jnp.bfloat16


def dot(a, b, ca, cb):
    return lax.dot_general(a, b, (((ca,), (cb,)), ((), ())), preferred_element_type=F32)


def attend(query, keys, values, d_mixed):
    row = lax.broadcasted_iota(jnp.int32, (2 * BLOCK, BLOCK), 0) % BLOCK
    col = lax.broadcasted_iota(jnp.int32, (2 * BLOCK, BLOCK), 1)
    visible = (row // BOOKS == col // BOOKS) & (col <= row)
    low = lax.broadcasted_iota(jnp.int32, (BLOCK, LANES), 1) < SIZE

    def stack(a):
        zero = jnp.zeros_like(a)
        return jnp.concatenate([jnp.where(low, a, zero), jnp.where(low, zero, a)], axis=0)

    def pick(a):
        return jnp.where(low, a[:BLOCK], a[BLOCK:]).astype(BF16)

    query, d_mixed = stack(query), stack(d_mixed)
    scores = dot(query, keys, 1, 1) * F32(0.125)
    weights = jnp.where(visible, jnp.exp(scores), F32(0.0))
    exact = weights * (F32(1.0) / jnp.sum(weights, axis=1, keepdims=True))
    probs = exact.astype(BF16)
    mixed = pick(dot(probs, values, 1, 0))
    d_probs = dot(d_mixed, values, 1, 1).astype(BF16).astype(F32)
    inner = jnp.sum(d_probs * exact, axis=1, keepdims=True)
    d_scores = (exact * (d_probs - inner) * F32(0.125)).astype(BF16)
    d_query = pick(dot(d_scores, keys, 1, 0))
    d_keys = dot(d_scores, query, 0, 0).astype(BF16)
    d_values = dot(probs, d_mixed, 0, 0).astype(BF16)
    return mixed, d_query, d_keys, d_values


def ring_place(axis):
    if axis == "y":
        return 2 * lax.axis_index("yh") + lax.axis_index("yl")
    return lax.axis_index(axis)


def ring_parts(axis):
    core, place = lax.axis_index("c"), ring_place(axis)
    first = jnp.where(core == 0, place ^ 1, 3 - place)
    second = jnp.where(core == 0, 3 - place, place ^ 1)
    return (first, place ^ 2, place, second)


def ring_pairs(axis, step):
    def index(place, core):
        if axis == "y":
            place = place % 2 * 2 + place // 2
        return 2 * place + core

    return [
        (index(p, c), index(p ^ 1 if c == step else 3 - p, c)) for p in range(4) for c in range(2)
    ]


def ring_shift(axis, shift):
    def index(place):
        return place % 2 * 2 + place // 2 if axis == "y" else place

    return [(index(p), index((p + shift) % 4)) for p in range(4)]


def ring_base(axis, place):
    if axis == "x":
        return place * 2
    if axis == "y":
        return place % 2 * 8 + place // 2
    return place * 16


def ring_rest(axis):
    if axis == "x":
        return [16 * z + 8 * yl + yh for z in range(4) for yl in range(2) for yh in range(2)]
    if axis == "y":
        return [16 * z + 2 * x for z in range(4) for x in range(4)]
    return list(range(16))


def positions():
    out = [lax.axis_index("c")]
    for axis in RING_ORDER:
        out += [ring_base(axis, place) for place in ring_parts(axis)]
    return jnp.stack(out).astype(jnp.int32)


def write_parts(at_ref, axis, give, keep, read):
    for part in range(4):
        out = give if part < 2 else keep
        for rest, offset in enumerate(ring_rest(axis)):
            chip = at_ref[1 + 4 * RING_ORDER.index(axis) + part] + offset
            row = (part % 2 * 16 + rest) * 16
            out[row : row + 16, :] = read(chip).astype(BF16)


class Stream:
    def __init__(self, give, keep, order):
        self.order = order
        self.sizes = [1 if name in RINGS[order[0].lower()] else size for name, size in CHIPS]
        self.give, self.keep, self.got = give, keep, None
        self.step, self.total = 0, None

    def send(self):
        axis = self.order[0]
        if axis.islower():
            self.got = [lax.ppermute(self.give, RINGS[axis] + ("c",), ring_pairs(axis, self.step))]
        else:
            axis = axis.lower()
            self.got = [
                lax.ppermute(give, RINGS[axis], ring_shift(axis, shift))
                for give, shift in zip(self.give, (2, 1, 3))
            ]

    def add(self):
        got, keep = [g.astype(F32) for g in self.got], self.keep.astype(F32)
        if self.order[0].islower() and self.step == 0:
            half = keep.shape[0] // 2
            self.keep = (keep[:half] + got[0][:half]).astype(BF16)
            self.give = (keep[half:] + got[0][half:]).astype(BF16)
            self.step = 1
            return
        total = sum(got, keep)
        self.step, self.order = 0, self.order[1:]
        if not self.order:
            self.total = total
        else:
            self.begin(total.astype(BF16))

    def begin(self, data):
        self.data = data
        axis = self.order[0].lower()
        width = data.shape[1]
        data = data.reshape(*self.sizes, 16, width)

        def part(place):
            out = data
            for dim, (name, _) in enumerate(CHIPS):
                if name in RINGS[axis]:
                    at = {"yl": place % 2, "yh": place // 2}.get(name, place)
                    out = lax.dynamic_slice_in_dim(out, at, 1, dim)
            return out.reshape(-1, width)

        if self.order[0].islower():
            first, third, mine, second = ring_parts(axis)
            self.give = jnp.concatenate([part(first), part(third)], axis=0)
            self.keep = jnp.concatenate([part(mine), part(second)], axis=0)
        else:
            place = ring_place(axis)
            self.give = [part(place ^ 2), part((place + 1) % 4), part((place + 3) % 4)]
            self.keep = part(place)
        self.sizes = [
            1 if name in RINGS[axis] else size for size, (name, _) in zip(self.sizes, CHIPS)
        ]


def join(a, b):
    out = Stream(None, None, a.order)
    out.sizes = [size if name in RINGS[a.order.lower()] else 1 for name, size in CHIPS]
    out.begin(jnp.concatenate([a.data, b.data], axis=1))
    return out


def together(streams, *values):
    out = lax.optimization_barrier(([s.got for s in streams], values))
    for s, got in zip(streams, out[0]):
        s.got = got
    return out[1]


def block_kernel(
    at_ref, emb_ref, ctx_ref, own_ref, oth_ref, wq_ref, wk_ref, wv_ref, wo_ref,
    d_flat_ref, d_ctx_ref, give_x, keep_x, give_z, keep_z,
    proj, d_proj, d_mixed, mixed, acc_qkv, acc_out,
):
    step = pl.program_id(0)
    rows, width = emb_ref.shape
    half = wq_ref.shape[1]
    stream = (
        emb_ref[...].astype(F32).reshape(rows // BOOKS, BOOKS, width)
        + ctx_ref[...].astype(F32)[:, None, :]
    ).reshape(rows, width).astype(BF16)
    cot = jnp.where(step < pl.num_programs(0) // 2, own_ref[...], oth_ref[...])
    for part, w_ref in enumerate((wq_ref, wk_ref, wv_ref)):
        proj[:, part * half : (part + 1) * half] = dot(stream, w_ref[...], 1, 0).astype(BF16)
    d_mixed[...] = dot(cot, wo_ref[...], 1, 1).astype(BF16)
    for block in range(rows // BLOCK):
        at = slice(block * BLOCK, (block + 1) * BLOCK)
        for pair in range(half // LANES):
            q = slice(pair * LANES, (pair + 1) * LANES)
            k = slice(half + pair * LANES, half + (pair + 1) * LANES)
            v = slice(2 * half + pair * LANES, 2 * half + (pair + 1) * LANES)
            mixed[at, q], d_proj[at, q], d_proj[at, k], d_proj[at, v] = attend(
                proj[at, q], proj[at, k], proj[at, v], d_mixed[at, q]
            )
    d_flat = dot(d_proj[:, :half], wq_ref[...], 1, 1)
    d_flat += dot(d_proj[:, half : 2 * half], wk_ref[...], 1, 1)
    d_flat += dot(d_proj[:, 2 * half :], wv_ref[...], 1, 1)
    d_flat_ref[...] = d_flat.astype(BF16)
    own = jnp.where(step < pl.num_programs(0) // 2, F32(1.0), F32(0.0))
    d_flat += cot.astype(F32) * own
    d_ctx_ref[...] = jnp.sum(d_flat.reshape(rows // BOOKS, BOOKS, width), axis=1).astype(BF16)

    @pl.when(step == 0)
    def _():
        acc_qkv[...] = dot(stream, d_proj[...], 0, 0)
        acc_out[...] = dot(mixed[...], cot, 0, 0)

    @pl.when(step > 0)
    def _():
        acc_qkv[...] += dot(stream, d_proj[...], 0, 0)
        acc_out[...] += dot(mixed[...], cot, 0, 0)

    @pl.when(step == pl.num_programs(0) - 1)
    def _():
        def qkv(chip, cols):
            return acc_qkv[pl.ds(pl.multiple_of(chip * 16, 16), 16), cols]

        def qk(chip):
            return qkv(chip, slice(0, 2 * half))

        def v_and_out(chip):
            start = pl.multiple_of((chip % 32 * 2 + chip // 32) * 8, 8)
            own = acc_out[pl.ds(start, 8), :]
            own = jnp.concatenate([own[:, :half], own[:, half:]], axis=0)
            return jnp.concatenate([qkv(chip, slice(2 * half, 3 * half)), own], axis=1)

        write_parts(at_ref, "x", give_x, keep_x, qk)
        write_parts(at_ref, "z", give_z, keep_z, v_and_out)


def halves(rows, width):
    last = 1
    return [
        pl.BlockSpec((rows, width), lambda i, *_: (jnp.minimum(i, last), 0)),
        pl.BlockSpec((rows, width), lambda i, *_: (jnp.maximum(i - last - 1, 0), 0)),
    ]


STEPS = 4


def block(at, embedded, context, own, oth, qkv_weight, out_weight):
    tokens, width = embedded.shape
    half = width // 2
    rows = tokens // STEPS
    tall = pl.BlockSpec((rows, width), lambda i, a: (i, 0))

    def third(part):
        return pl.BlockSpec((width, half), lambda i, a: (0, 2 * part + a[0]))

    out = (width // 2, width)
    return pl.pallas_call(
        block_kernel,
        grid_spec=pltpu.PrefetchScalarGridSpec(
            num_scalar_prefetch=1,
            grid=(STEPS,),
            in_specs=[
                tall,
                pl.BlockSpec((rows // BOOKS, width), lambda i, a: (i, 0)),
                *halves(rows, width),
                third(0),
                third(1),
                third(2),
                pl.BlockSpec((half, width), lambda i, a: (a[0], 0)),
            ],
            out_specs=[
                tall,
                pl.BlockSpec(
                    (rows // BOOKS, width), lambda i, a: ((i + STEPS // 2 * a[0]) % STEPS, 0)
                ),
            ]
            + [pl.BlockSpec(out, lambda i, a: (0, 0))] * 4,
            scratch_shapes=[
                pltpu.VMEM((rows, 3 * half), BF16),
                pltpu.VMEM((rows, 3 * half), BF16),
                pltpu.VMEM((rows, half), BF16),
                pltpu.VMEM((rows, half), BF16),
                pltpu.VMEM((width, 3 * half), F32),
                pltpu.VMEM((half, width), F32),
            ],
        ),
        out_shape=[
            jax.ShapeDtypeStruct((tokens, width), BF16),
            jax.ShapeDtypeStruct((tokens // BOOKS, width), BF16),
        ]
        + [jax.ShapeDtypeStruct(out, BF16)] * 4,
        compiler_params=pltpu.CompilerParams(vmem_limit_bytes=48 * 1024 * 1024),
        cost_estimate=pl.CostEstimate(
            flops=22 * tokens * width * width // 2,
            bytes_accessed=20 * 1024 * 1024,
            transcendentals=tokens * BLOCK * half // SIZE,
        ),
    )(at, embedded, context, own, oth, qkv_weight, qkv_weight, qkv_weight, out_weight)


def table_kernel(at_ref, ids_ref, own_ref, oth_ref, mine_ref, other_ref, d_table_ref, acc):
    step = pl.program_id(0)
    cot = jnp.where(step < pl.num_programs(0) // 2, own_ref[...], oth_ref[...])
    d_flat = (mine_ref[...].astype(F32) + other_ref[...].astype(F32)).astype(BF16)
    d_stream = (cot.astype(F32) + d_flat.astype(F32)).astype(BF16)
    place = lax.broadcasted_iota(jnp.int32, (acc.shape[0], d_stream.shape[0]), 0)
    row = place // 16 * 32 + at_ref[0] * 16 + place % 16
    onehot = jnp.where(row == ids_ref[...], F32(1.0), F32(0.0)).astype(BF16)
    part = dot(onehot, d_stream, 1, 0)

    @pl.when(step == 0)
    def _():
        acc[...] = part

    @pl.when(step > 0)
    def _():
        acc[...] += part

    @pl.when(step == pl.num_programs(0) - 1)
    def _():
        d_table_ref[...] = acc[...].astype(BF16)


def table_grad(at, ids, own, oth, mine, other, vocab):
    tokens, width = mine.shape
    rows = tokens // STEPS
    out = (vocab // 2, width)
    return pl.pallas_call(
        table_kernel,
        grid_spec=pltpu.PrefetchScalarGridSpec(
            num_scalar_prefetch=1,
            grid=(STEPS,),
            in_specs=[
                pl.BlockSpec((1, rows), lambda i, a: (0, i)),
                *halves(rows, width),
                pl.BlockSpec((rows, width), lambda i, a: (i, 0)),
                pl.BlockSpec((rows, width), lambda i, a: ((i + STEPS // 2) % STEPS, 0)),
            ],
            out_specs=pl.BlockSpec(out, lambda i, a: (0, 0)),
            scratch_shapes=[pltpu.VMEM(out, F32)],
        ),
        out_shape=jax.ShapeDtypeStruct(out, BF16),
        compiler_params=pltpu.CompilerParams(vmem_limit_bytes=32 * 1024 * 1024),
        cost_estimate=pl.CostEstimate(
            flops=tokens * width * vocab, bytes_accessed=9 * tokens * width, transcendentals=0
        ),
    )(at, ids, own, oth, mine, other)


def on_device(hidden, ctx_weight, codes, table, qkv_weight, out_weight, cotangent):
    core = lax.axis_index("c")
    yh = lax.axis_index("yh")
    width = ctx_weight.shape[1]
    half = width // 2
    frames = codes.shape[0]
    tokens = 2 * frames * BOOKS
    vocab = table.shape[0]
    at = positions()

    partial_ctx = dot(hidden, ctx_weight, 1, 0).astype(BF16).reshape(2, 2 * frames, width)
    away = lax.dynamic_index_in_dim(partial_ctx, 1 - yh, 0, keepdims=False)
    near = lax.dynamic_index_in_dim(partial_ctx, yh, 0, keepdims=False)
    far = lax.ppermute(away, "yh", SWAP)

    swap = functools.partial(lax.ppermute, axis_name="c", perm=SWAP)
    ids = jnp.concatenate([codes, swap(codes)], axis=0).reshape(tokens)
    own = cotangent.reshape(frames * BOOKS, width)
    oth = swap(own)
    onehot = (ids[:, None] == jnp.arange(vocab, dtype=jnp.int32)[None, :]).astype(BF16)
    embedded = dot(onehot, table, 1, 0).astype(BF16)

    far, embedded, oth = lax.optimization_barrier((far, embedded, oth))
    chip_ctx = (near.astype(F32) + far.astype(F32)).astype(BF16)
    context = (chip_ctx.astype(F32) + swap(chip_ctx).astype(F32)).astype(BF16)
    context = jnp.where(core == 0, context, jnp.roll(context, frames, axis=0))

    d_flat, d_ctx, give_x, keep_x, give_z, keep_z = block(
        at, embedded, context, own, oth, qkv_weight, out_weight
    )
    d_ctx = (d_ctx.astype(F32) + swap(d_ctx).astype(F32)).astype(BF16)
    d_ctx_far = lax.ppermute(d_ctx, "yh", SWAP)
    qk, vo = Stream(give_x, keep_x, "xzY"), Stream(give_z, keep_z, "zxY")
    for s in (qk, vo):
        s.send()
    other = swap(d_flat)
    d_ctx, d_ctx_far, other = together([qk, vo], d_ctx, d_ctx_far, other)

    d_ctx = jnp.where(
        yh == 0,
        jnp.concatenate([d_ctx, d_ctx_far], axis=0),
        jnp.concatenate([d_ctx_far, d_ctx], axis=0),
    )
    ctx_part = dot(hidden, d_ctx, 0, 0).astype(BF16)
    arrived = lax.all_to_all(ctx_part.reshape(32, 32, width), SEQ, 0, 0, tiled=False)
    for s in (qk, vo):
        s.add()
        s.send()
    d_table = table_grad(at, ids.reshape(1, tokens), own, oth, d_flat, other, vocab)
    arrived, d_table = together([qk, vo], arrived, d_table)

    got_table = lax.all_to_all(d_table.reshape(64, 16, width), ALL[:4], 0, 0, tiled=False)
    ctx_sum = jnp.sum(arrived.astype(F32), axis=0).astype(BF16)
    spread = jnp.broadcast_to(ctx_sum[None], (32, 32, width))
    for s in (qk, vo):
        s.add()
        s.send()
    got_table, spread = together([qk, vo], got_table, spread)

    grad_ctx = lax.all_to_all(spread, SEQ, 0, 0, tiled=False).reshape(32 * 32, width).astype(F32)
    grad_table = jnp.sum(got_table.astype(F32), axis=0)
    for s in (qk, vo):
        s.add()
        s.send()
    for s in (qk, vo):
        s.add()
    both = join(qk, vo)
    both.send()
    both.add()
    d_hidden = dot(d_ctx, ctx_weight, 1, 1).astype(BF16)

    sum_qkv, sum_out = both.total[:, : 3 * half], both.total[:, 3 * half :]
    sum_out = jnp.concatenate([sum_out[:8], sum_out[8:]], axis=1)
    grad_out = lax.ppermute(
        sum_out, ("z", "c"), [(2 * z + c, 2 * (2 * c + z % 2) + z // 2) for z in range(4) for c in range(2)]
    )
    keep = lax.dynamic_slice_in_dim(sum_qkv, core * 8, 8, 0)
    give = lax.dynamic_slice_in_dim(sum_qkv, 8 - core * 8, 8, 0)
    take = swap(give)
    keep, take = keep.reshape(8, 3, 1, half), take.reshape(8, 3, 1, half)
    grad_qkv = jnp.where(
        core == 0, jnp.concatenate([keep, take], axis=2), jnp.concatenate([take, keep], axis=2)
    ).reshape(8, 6 * half)
    return (d_hidden, grad_ctx, grad_table, grad_qkv, grad_out)


def solution(mesh):
    fine = Mesh(mesh.devices.reshape(4, 2, 4, 2, 2), ALL)
    in_specs = (
        P(SEQ, ("yh", "c")),
        P(("yh", "c"), None),
        P(ALL, None),
        P(),
        P(),
        P(),
        P(ALL, None, None),
    )
    out_specs = (
        P(SEQ, ("yh", "c")),
        P(("yh", "c"), None),
        P(ALL, None),
        P(ALL, None),
        P(ALL, None),
    )
    return jax.shard_map(
        on_device, mesh=fine, in_specs=in_specs, out_specs=out_specs, check_vma=False
    )
```

```python
import functools

import jax
import jax.numpy as jnp
from jax import lax
from jax.experimental import pallas as pl
from jax.experimental.pallas import tpu as pltpu
from jax.sharding import Mesh, PartitionSpec as P

HEADS = 16
BOOKS = 8
SIZE = 64
LANES = 128
BLOCK = 128

ALL = ("z", "yl", "x", "yh", "c")
SEQ = ("z", "yl", "x")
SWAP = [(0, 1), (1, 0)]

CHIPS = (("z", 4), ("yl", 2), ("x", 4), ("yh", 2))
RINGS = {"x": ("x",), "y": ("yl", "yh"), "z": ("z",)}
RING_ORDER = ("x", "y", "z")
F32 = jnp.float32
BF16 = jnp.bfloat16


def dot(a, b, ca, cb):
    return lax.dot_general(a, b, (((ca,), (cb,)), ((), ())), preferred_element_type=F32)


def attend(proj, d_mixed, mixed, d_proj, at):
    half = d_mixed.shape[1]
    low = lax.broadcasted_iota(jnp.int32, (BLOCK, LANES), 1) < SIZE
    group = lax.broadcasted_iota(jnp.int32, (BOOKS, 2 * BLOCK), 1) % BLOCK // BOOKS
    frames = BLOCK // BOOKS

    def stack(a):
        zero = jnp.zeros_like(a)
        return jnp.concatenate([jnp.where(low, a, zero), jnp.where(low, zero, a)], axis=0)

    def pick(a):
        return jnp.where(low, a[:BLOCK], a[BLOCK:]).astype(BF16)

    def gather(a):
        out = a[:BOOKS]
        for f in range(1, frames):
            out = jnp.where(group == f, a[f * BOOKS : (f + 1) * BOOKS], out)
        return out

    def spread(a):
        zero = jnp.zeros_like(a)
        return jnp.concatenate(
            [jnp.where(group == f, a, zero) for f in range(frames)], axis=0
        ).astype(BF16)

    pairs = half // LANES
    cols = [slice(p * LANES, (p + 1) * LANES) for p in range(pairs)]
    kcols = [slice(half + c.start, half + c.stop) for c in cols]
    vcols = [slice(2 * half + c.start, 2 * half + c.stop) for c in cols]
    scores = [gather(dot(proj[at, k], stack(proj[at, q]), 1, 1)) for q, k in zip(cols, kcols)]
    d_probs = [gather(dot(proj[at, v], stack(d_mixed[at, q]), 1, 1)) for q, v in zip(cols, vcols)]
    scores = jnp.concatenate(scores, axis=1) * F32(0.125)
    d_probs = jnp.concatenate(d_probs, axis=1).astype(BF16).astype(F32)
    key = lax.broadcasted_iota(jnp.int32, scores.shape, 0)
    query = lax.broadcasted_iota(jnp.int32, scores.shape, 1) % BOOKS
    weights = jnp.where(key <= query, jnp.exp(scores), F32(0.0))
    exact = weights / jnp.sum(weights, axis=0, keepdims=True)
    inner = jnp.sum(d_probs * exact, axis=0, keepdims=True)
    d_scores = exact * (d_probs - inner) * F32(0.125)
    for p in range(pairs):
        here = slice(p * 2 * BLOCK, (p + 1) * 2 * BLOCK)
        probs = spread(exact[:, here])
        mixed[at, cols[p]] = pick(dot(probs, proj[at, vcols[p]], 0, 0))
        d_proj[at, vcols[p]] = dot(probs, stack(d_mixed[at, cols[p]]), 1, 0).astype(BF16)
        ds = spread(d_scores[:, here])
        d_proj[at, cols[p]] = pick(dot(ds, proj[at, kcols[p]], 0, 0))
        d_proj[at, kcols[p]] = dot(ds, stack(proj[at, cols[p]]), 1, 0).astype(BF16)


def ring_place(axis):
    if axis == "y":
        return 2 * lax.axis_index("yh") + lax.axis_index("yl")
    return lax.axis_index(axis)


def ring_parts(axis):
    core, place = lax.axis_index("c"), ring_place(axis)
    first = jnp.where(core == 0, place ^ 1, 3 - place)
    second = jnp.where(core == 0, 3 - place, place ^ 1)
    return (first, place ^ 2, place, second)


def ring_pairs(axis, step):
    def index(place, core):
        if axis == "y":
            place = place % 2 * 2 + place // 2
        return 2 * place + core

    return [
        (index(p, c), index(p ^ 1 if c == step else 3 - p, c)) for p in range(4) for c in range(2)
    ]


def ring_shift(axis, shift):
    def index(place):
        return place % 2 * 2 + place // 2 if axis == "y" else place

    return [(index(p), index((p + shift) % 4)) for p in range(4)]


def ring_base(axis, place):
    if axis == "x":
        return place * 2
    if axis == "y":
        return place % 2 * 8 + place // 2
    return place * 16


def ring_rest(axis):
    if axis == "x":
        return [16 * z + 8 * yl + yh for z in range(4) for yl in range(2) for yh in range(2)]
    if axis == "y":
        return [16 * z + 2 * x for z in range(4) for x in range(4)]
    return list(range(16))


def positions():
    out = [lax.axis_index("c")]
    for axis in RING_ORDER:
        out += [ring_base(axis, place) for place in ring_parts(axis)]
    return jnp.stack(out).astype(jnp.int32)


def write_parts(at_ref, axis, give, keep, read):
    for part in range(4):
        out = give if part < 2 else keep
        for rest, offset in enumerate(ring_rest(axis)):
            chip = at_ref[1 + 4 * RING_ORDER.index(axis) + part] + offset
            row = (part % 2 * 16 + rest) * 16
            out[row : row + 16, :] = read(chip).astype(BF16)


class Stream:
    def __init__(self, give, keep, order):
        self.order = order
        self.sizes = [1 if name in RINGS[order[0].lower()] else size for name, size in CHIPS]
        self.give, self.keep, self.got = give, keep, None
        self.step, self.total = 0, None

    def send(self):
        axis = self.order[0]
        if axis.islower():
            self.got = [lax.ppermute(self.give, RINGS[axis] + ("c",), ring_pairs(axis, self.step))]
        else:
            axis = axis.lower()
            self.got = [
                lax.ppermute(give, RINGS[axis], ring_shift(axis, shift))
                for give, shift in zip(self.give, (2, 1, 3))
            ]

    def add(self):
        got, keep = self.got, self.keep
        if self.order[0].islower() and self.step == 0:
            half = keep.shape[0] // 2
            self.keep = (keep[:half].astype(F32) + got[0][:half].astype(F32)).astype(BF16)
            self.give = (keep[half:].astype(F32) + got[0][half:].astype(F32)).astype(BF16)
            self.step = 1
            return
        total = sum([g.astype(F32) for g in got], keep.astype(F32))
        self.step, self.order = 0, self.order[1:]
        if not self.order:
            self.total = total
        else:
            self.begin(total.astype(BF16))

    def begin(self, data):
        self.data = data
        axis = self.order[0].lower()
        width = data.shape[1]
        data = data.reshape(*self.sizes, 16, width)

        def part(place):
            out = data
            for dim, (name, _) in enumerate(CHIPS):
                if name in RINGS[axis]:
                    at = {"yl": place % 2, "yh": place // 2}.get(name, place)
                    out = lax.dynamic_slice_in_dim(out, at, 1, dim)
            return out.reshape(-1, width)

        if self.order[0].islower():
            first, third, mine, second = ring_parts(axis)
            self.give = jnp.concatenate([part(first), part(third)], axis=0)
            self.keep = jnp.concatenate([part(mine), part(second)], axis=0)
        else:
            place = ring_place(axis)
            self.give = [part(place ^ 2), part((place + 1) % 4), part((place + 3) % 4)]
            self.keep = part(place)
        self.sizes = [
            1 if name in RINGS[axis] else size for size, (name, _) in zip(self.sizes, CHIPS)
        ]


def join(a, b):
    out = Stream(None, None, a.order)
    out.sizes = [size if name in RINGS[a.order.lower()] else 1 for name, size in CHIPS]
    out.begin(jnp.concatenate([a.data, b.data], axis=1))
    return out


def together(streams, *values):
    out = lax.optimization_barrier(([s.got for s in streams], values))
    for s, got in zip(streams, out[0]):
        s.got = got
    return out[1]


def after(streams, value):
    for s in streams:
        s.got, _ = lax.optimization_barrier((s.got, value))


def block_kernel(
    at_ref, emb_ref, ctx_ref, own_ref, oth_ref, wq_ref, wk_ref, wv_ref, wo_ref,
    d_flat_ref, d_ctx_ref, give_x, keep_x, give_z, keep_z,
    proj, d_proj, d_mixed, mixed, acc_qkv, acc_out,
):
    step = pl.program_id(0)
    rows, width = emb_ref.shape
    half = wq_ref.shape[1]
    stream = (
        emb_ref[...].astype(F32).reshape(rows // BOOKS, BOOKS, width)
        + ctx_ref[...].astype(F32)[:, None, :]
    ).reshape(rows, width).astype(BF16)
    cot = jnp.where(step < pl.num_programs(0) // 2, own_ref[...], oth_ref[...])
    for part, w_ref in enumerate((wq_ref, wk_ref, wv_ref)):
        proj[:, part * half : (part + 1) * half] = dot(stream, w_ref[...], 1, 0).astype(BF16)
    d_mixed[...] = dot(cot, wo_ref[...], 1, 1).astype(BF16)
    for block in range(rows // BLOCK):
        attend(proj, d_mixed, mixed, d_proj, slice(block * BLOCK, (block + 1) * BLOCK))
    d_flat = dot(d_proj[:, :half], wq_ref[...], 1, 1)
    d_flat += dot(d_proj[:, half : 2 * half], wk_ref[...], 1, 1)
    d_flat += dot(d_proj[:, 2 * half :], wv_ref[...], 1, 1)
    d_flat_ref[...] = d_flat.astype(BF16)
    own = jnp.where(step < pl.num_programs(0) // 2, F32(1.0), F32(0.0))
    d_flat += cot.astype(F32) * own
    d_ctx_ref[...] = jnp.sum(d_flat.reshape(rows // BOOKS, BOOKS, width), axis=1).astype(BF16)

    @pl.when(step == 0)
    def _():
        acc_qkv[...] = dot(stream, d_proj[...], 0, 0)
        acc_out[...] = dot(mixed[...], cot, 0, 0)

    @pl.when(step > 0)
    def _():
        acc_qkv[...] += dot(stream, d_proj[...], 0, 0)
        acc_out[...] += dot(mixed[...], cot, 0, 0)

    @pl.when(step == pl.num_programs(0) - 1)
    def _():
        def qkv(chip, cols):
            return acc_qkv[pl.ds(pl.multiple_of(chip * 16, 16), 16), cols]

        def qk(chip):
            return qkv(chip, slice(0, 2 * half))

        def v_and_out(chip):
            start = pl.multiple_of((chip % 32 * 2 + chip // 32) * 8, 8)
            own = acc_out[pl.ds(start, 8), :]
            own = jnp.concatenate([own[:, :half], own[:, half:]], axis=0)
            return jnp.concatenate([qkv(chip, slice(2 * half, 3 * half)), own], axis=1)

        write_parts(at_ref, "x", give_x, keep_x, qk)
        write_parts(at_ref, "z", give_z, keep_z, v_and_out)


def halves(rows, width):
    last = STEPS // 2 - 1
    return [
        pl.BlockSpec((rows, width), lambda i, *_: (jnp.minimum(i, last), 0)),
        pl.BlockSpec((rows, width), lambda i, *_: (jnp.maximum(i - last - 1, 0), 0)),
    ]


STEPS = 4


def block(at, embedded, context, own, oth, qkv_weight, out_weight):
    tokens, width = embedded.shape
    half = width // 2
    rows = tokens // STEPS
    tall = pl.BlockSpec((rows, width), lambda i, a: (i, 0))

    def third(part):
        return pl.BlockSpec((width, half), lambda i, a: (0, 2 * part + a[0]))

    out = (width // 2, width)
    return pl.pallas_call(
        block_kernel,
        grid_spec=pltpu.PrefetchScalarGridSpec(
            num_scalar_prefetch=1,
            grid=(STEPS,),
            in_specs=[
                tall,
                pl.BlockSpec((rows // BOOKS, width), lambda i, a: (i, 0)),
                *halves(rows, width),
                third(0),
                third(1),
                third(2),
                pl.BlockSpec((half, width), lambda i, a: (a[0], 0)),
            ],
            out_specs=[
                tall,
                pl.BlockSpec(
                    (rows // BOOKS, width), lambda i, a: ((i + STEPS // 2 * a[0]) % STEPS, 0)
                ),
            ]
            + [pl.BlockSpec(out, lambda i, a: (0, 0))] * 4,
            scratch_shapes=[
                pltpu.VMEM((rows, 3 * half), BF16),
                pltpu.VMEM((rows, 3 * half), BF16),
                pltpu.VMEM((rows, half), BF16),
                pltpu.VMEM((rows, half), BF16),
                pltpu.VMEM((width, 3 * half), F32),
                pltpu.VMEM((half, width), F32),
            ],
        ),
        out_shape=[
            jax.ShapeDtypeStruct((tokens, width), BF16),
            jax.ShapeDtypeStruct((tokens // BOOKS, width), BF16),
        ]
        + [jax.ShapeDtypeStruct(out, BF16)] * 4,
        compiler_params=pltpu.CompilerParams(vmem_limit_bytes=48 * 1024 * 1024),
        cost_estimate=pl.CostEstimate(
            flops=22 * tokens * width * width // 2,
            bytes_accessed=20 * 1024 * 1024,
            transcendentals=tokens * BLOCK * half // SIZE,
        ),
    )(at, embedded, context, own, oth, qkv_weight, qkv_weight, qkv_weight, out_weight)


def table_kernel(at_ref, ids_ref, own_ref, oth_ref, mine_ref, other_ref, give_ref, keep_ref, acc):
    step = pl.program_id(0)
    cot = jnp.where(step < pl.num_programs(0) // 2, own_ref[...], oth_ref[...])
    d_flat = (mine_ref[...].astype(F32) + other_ref[...].astype(F32)).astype(BF16)
    d_stream = (cot.astype(F32) + d_flat.astype(F32)).astype(BF16)
    place = lax.broadcasted_iota(jnp.int32, (acc.shape[0], d_stream.shape[0]), 0)
    row = place // 16 * 32 + at_ref[0] * 16 + place % 16
    onehot = jnp.where(row == ids_ref[...], F32(1.0), F32(0.0)).astype(BF16)
    part = dot(onehot, d_stream, 1, 0)

    @pl.when(step == 0)
    def _():
        acc[...] = part

    @pl.when(step > 0)
    def _():
        acc[...] += part

    @pl.when(step == pl.num_programs(0) - 1)
    def _():
        def read(chip):
            return acc[pl.ds(pl.multiple_of(chip * 16, 16), 16), :]

        write_parts(at_ref, "y", give_ref, keep_ref, read)


def table_grad(at, ids, own, oth, mine, other, vocab):
    tokens, width = mine.shape
    rows = tokens // STEPS
    out = (vocab // 4, width)
    return pl.pallas_call(
        table_kernel,
        grid_spec=pltpu.PrefetchScalarGridSpec(
            num_scalar_prefetch=1,
            grid=(STEPS,),
            in_specs=[
                pl.BlockSpec((1, rows), lambda i, a: (0, i)),
                *halves(rows, width),
                pl.BlockSpec((rows, width), lambda i, a: (i, 0)),
                pl.BlockSpec((rows, width), lambda i, a: ((i + STEPS // 2) % STEPS, 0)),
            ],
            out_specs=[pl.BlockSpec(out, lambda i, a: (0, 0))] * 2,
            scratch_shapes=[pltpu.VMEM((vocab // 2, width), F32)],
        ),
        out_shape=[jax.ShapeDtypeStruct(out, BF16)] * 2,
        compiler_params=pltpu.CompilerParams(vmem_limit_bytes=56 * 1024 * 1024),
        cost_estimate=pl.CostEstimate(
            flops=tokens * width * vocab, bytes_accessed=9 * tokens * width, transcendentals=0
        ),
    )(at, ids, own, oth, mine, other)


def on_device(hidden, ctx_weight, codes, table, qkv_weight, out_weight, cotangent):
    core = lax.axis_index("c")
    yh = lax.axis_index("yh")
    width = ctx_weight.shape[1]
    half = width // 2
    frames = codes.shape[0]
    tokens = 2 * frames * BOOKS
    vocab = table.shape[0]
    at = positions()

    partial_ctx = dot(hidden, ctx_weight, 1, 0).astype(BF16).reshape(2, 2 * frames, width)
    away = lax.dynamic_index_in_dim(partial_ctx, 1 - yh, 0, keepdims=False)
    near = lax.dynamic_index_in_dim(partial_ctx, yh, 0, keepdims=False)
    far = lax.ppermute(away, "yh", SWAP)

    swap = functools.partial(lax.ppermute, axis_name="c", perm=SWAP)
    ids = jnp.concatenate([codes, swap(codes)], axis=0).reshape(tokens)
    own = cotangent.reshape(frames * BOOKS, width)
    oth = swap(own)
    onehot = (ids[:, None] == jnp.arange(vocab, dtype=jnp.int32)[None, :]).astype(BF16)
    embedded = dot(onehot, table, 1, 0).astype(BF16)

    far, embedded, oth = lax.optimization_barrier((far, embedded, oth))
    chip_ctx = (near.astype(F32) + far.astype(F32)).astype(BF16)
    context = (chip_ctx.astype(F32) + swap(chip_ctx).astype(F32)).astype(BF16)
    context = jnp.where(core == 0, context, jnp.roll(context, frames, axis=0))

    d_flat, d_ctx, give_x, keep_x, give_z, keep_z = block(
        at, embedded, context, own, oth, qkv_weight, out_weight
    )
    d_ctx = (d_ctx.astype(F32) + swap(d_ctx).astype(F32)).astype(BF16)
    qk, vo = Stream(give_x, keep_x, "xzY"), Stream(give_z, keep_z, "zxY")
    qk.give, vo.give, d_flat, d_ctx = lax.optimization_barrier((qk.give, vo.give, d_flat, d_ctx))
    d_ctx_far = lax.ppermute(d_ctx, "yh", SWAP)
    for s in (qk, vo):
        s.send()
    other = swap(d_flat)
    parts = table_grad(at, ids.reshape(1, tokens), own, oth, d_flat, other, vocab)
    parts, d_ctx, d_ctx_far = together([qk, vo], parts, d_ctx, d_ctx_far)
    rows = Stream(*parts, "yXZ")
    streams = [qk, vo, rows]
    rows.send()
    for s in (qk, vo):
        s.add()
        s.send()
    d_ctx = jnp.where(
        yh == 0,
        jnp.concatenate([d_ctx, d_ctx_far], axis=0),
        jnp.concatenate([d_ctx_far, d_ctx], axis=0),
    )
    ctx_part = dot(hidden, d_ctx, 0, 0).astype(BF16).reshape(32, 32, width)
    (ctx_part,) = together(streams, ctx_part)
    arrived = lax.all_to_all(ctx_part, SEQ, 0, 0, tiled=False)
    for s in streams:
        s.add()
        s.send()
    ctx_sum = jnp.sum(arrived.astype(F32), axis=0).astype(BF16)
    spread = jnp.broadcast_to(ctx_sum[None], (32, 32, width))
    (spread,) = together(streams, spread)
    grad_ctx = lax.all_to_all(spread, SEQ, 0, 0, tiled=False).reshape(32 * 32, width).astype(F32)
    for s in streams:
        s.add()
        s.send()
    after(streams, grad_ctx[:8, :128])
    for s in (qk, vo):
        s.add()
    both = join(qk, vo)
    both.send()
    rows.add()
    rows.send()
    both.add()
    rows.add()
    grad_table = rows.total
    d_hidden = dot(d_ctx, ctx_weight, 1, 1).astype(BF16)

    sum_qkv, sum_out = both.total[:, : 3 * half], both.total[:, 3 * half :]
    sum_out = jnp.concatenate([sum_out[:8], sum_out[8:]], axis=1)
    grad_out = lax.ppermute(
        sum_out, ("z", "c"), [(2 * z + c, 2 * (2 * c + z % 2) + z // 2) for z in range(4) for c in range(2)]
    )
    keep = lax.dynamic_slice_in_dim(sum_qkv, core * 8, 8, 0)
    give = lax.dynamic_slice_in_dim(sum_qkv, 8 - core * 8, 8, 0)
    take = swap(give)
    keep, take = keep.reshape(8, 3, 1, half), take.reshape(8, 3, 1, half)
    grad_qkv = jnp.where(
        core == 0, jnp.concatenate([keep, take], axis=2), jnp.concatenate([take, keep], axis=2)
    ).reshape(8, 6 * half)
    return (d_hidden, grad_ctx, grad_table, grad_qkv, grad_out)


def solution(mesh):
    fine = Mesh(mesh.devices.reshape(4, 2, 4, 2, 2), ALL)
    in_specs = (
        P(SEQ, ("yh", "c")),
        P(("yh", "c"), None),
        P(ALL, None),
        P(),
        P(),
        P(),
        P(ALL, None, None),
    )
    out_specs = (
        P(SEQ, ("yh", "c")),
        P(("yh", "c"), None),
        P(ALL, None),
        P(ALL, None),
        P(ALL, None),
    )
    return jax.shard_map(
        on_device, mesh=fine, in_specs=in_specs, out_specs=out_specs, check_vma=False
    )
```
